32 devices in a mesh: groups: 2 (over y), ctx: 4 (over z), mp: 4 (over x, core).
Axes of the slice: x: 2, y: 2, z: 4, core: 2. Of those that a mesh axis runs over, the one named last changes fastest.
Arguments:
- query: bfloat16 [4096, 8192], P(('groups', 'ctx'), 'mp'), parts along dimension 0, may hold values from -200 to 200
- span_keys: bfloat16 [4096, 1024], P(('groups', 'ctx'), 'mp'), parts along dimension 0, may hold values from -6 to 6
- span_values: bfloat16 [4096, 1024], P(('groups', 'ctx'), 'mp'), parts along dimension 0, may hold values from -6 to 6
- cache_keys: bfloat16 [8192, 1024], P(('groups', 'ctx'), 'mp'), parts along dimension 0, may hold values from -13 to 13
- stored_values: bfloat16 [8192, 1024], P(('groups', 'ctx'), 'mp'), parts along dimension 0, may hold values from -6 to 6
- selected: int32 [8, 8, 2], P(('groups', 'ctx'), 'mp'), parts along dimension 0, may hold values from 0 to 7, as said below
Outputs:
- attended: bfloat16 [4096, 8192], P(('groups', 'ctx'), 'mp'), parts along dimension 0
The draws below stay inside these ranges and needn't reach their ends.
There are 2 independent parts, one for each index of `groups`. The reference program is written for one: setup_inputs(seed, part) draws one part's arguments, and reference() takes and returns one part's arrays. A program takes and returns all parts, laid end to end along the dimension named above; each array names one. Nothing has to cross between parts.
Inputs may be any that keep to these rules, and one draw needn't show every extreme that they name: `selected`: the two blocks chosen for a query block and key head lie in different ranges of 2 consecutive blocks, starting at multiples of 2.
All inputs are finite; a program needn't handle non-finite values.
Results may differ from the reference program's by a relative error of at most 0.0047.
Values may be sent and summed in bfloat16 or wider, within the bound.
A program may use at most 64 MiB of HBM per device.

```python
import jax
import jax.numpy as jnp
from jax import lax

QUERY_HEADS = 64
KEY_VALUE_HEADS = 8
HEAD_DIMENSION = 128
BLOCK = 512
BLOCKS_PER_OWNER = 2
QUERY_BLOCKS = 4
SPAN_POSITIONS = 2048
CACHED_POSITIONS = 4096


def draw_query(key, part):
    regular_portion = jnp.clip(jax.random.normal(key, (SPAN_POSITIONS, QUERY_HEADS * HEAD_DIMENSION), jnp.float32), -6.0, 6.0)
    return regular_portion.astype(jnp.bfloat16)


def draw_cache_keys(key, part):
    regular_portion = jnp.clip(jax.random.normal(key, (CACHED_POSITIONS, KEY_VALUE_HEADS * HEAD_DIMENSION), jnp.float32), -6.0, 6.0)
    return regular_portion.astype(jnp.bfloat16)


def draw_selected(key, part):
    holder_count = CACHED_POSITIONS // (BLOCK * BLOCKS_PER_OWNER)
    leading_key, trailing_key, nested_key = jax.random.split(key, 3)
    leading_holder = jax.random.randint(leading_key, (QUERY_BLOCKS, KEY_VALUE_HEADS), 0, holder_count)
    trailing_holder = (leading_holder + jax.random.randint(trailing_key, (QUERY_BLOCKS, KEY_VALUE_HEADS), 1, holder_count)) % holder_count
    nested_block = jax.random.randint(nested_key, (QUERY_BLOCKS, KEY_VALUE_HEADS, 2), 0, BLOCKS_PER_OWNER)
    return (jnp.stack([leading_holder, trailing_holder], axis=-1) * BLOCKS_PER_OWNER + nested_block).astype(jnp.int32)


def block_scale(rng, extent, cuts, smallest, largest):
    loudness = 1.0
    for axis_at, blocks in cuts:
        heights = jax.random.uniform(jax.random.fold_in(jax.random.fold_in(rng, 6), axis_at), (blocks,), jnp.float32, smallest / len(cuts), largest / len(cuts))
        loudness = loudness * jnp.repeat(jnp.exp(heights), extent[axis_at] // blocks).reshape((-1,) + (1,) * (len(extent) - 1 - axis_at))
    return loudness


def gaussian(rng, shape, deviation, most, shards=(), kind=jnp.bfloat16):
    loudness = block_scale(rng, shape, shards, -0.22, 0.18) if shards else 1.0
    entries = jax.random.normal(rng, shape, jnp.float32) * deviation * loudness
    return jnp.minimum(jnp.maximum(entries, -most), most).astype(kind)


def setup_inputs(seed: int = 0, part: int = 0) -> dict:
    streams_of = jax.random.split(jax.random.key(seed), 7)
    own_keys = jax.random.split(jax.random.fold_in(streams_of[6], part), 7)
    return {
        "query": draw_query(jax.random.fold_in(jax.random.fold_in(streams_of[6], part), 71), part),
        "span_keys": gaussian(own_keys[1], (SPAN_POSITIONS, KEY_VALUE_HEADS * HEAD_DIMENSION), 1.0, 6.0, ((0, 4), (1, 4))),
        "span_values": gaussian(own_keys[2], (SPAN_POSITIONS, KEY_VALUE_HEADS * HEAD_DIMENSION), 1.0, 6.0, ((0, 4), (1, 4))),
        "cache_keys": draw_cache_keys(jax.random.fold_in(jax.random.fold_in(streams_of[6], part), 71), part),
        "stored_values": gaussian(own_keys[4], (CACHED_POSITIONS, KEY_VALUE_HEADS * HEAD_DIMENSION), 1.0, 6.0, ((0, 4), (1, 4))),
        "selected": draw_selected(jax.random.fold_in(jax.random.fold_in(streams_of[6], part), 71), part),
    }


def attend(query_group, all_keys, all_values, query_group_count):
    block_rows = query_group.shape[0]
    head_size = all_keys.shape[1]
    score_scale = head_size ** -0.5
    query_pos = jnp.arange(block_rows, dtype=jnp.int32)[:, None]
    key_pos = jnp.arange(all_keys.shape[0], dtype=jnp.int32)[None, :]
    visible = (key_pos >= block_rows) | (key_pos <= query_pos)
    results = []
    for member in range(query_group_count):
        query_head = query_group[:, member * head_size:(member + 1) * head_size]
        scores = jnp.dot(query_head, all_keys.T, preferred_element_type=jnp.float32) * score_scale
        scores = jnp.where(visible, scores, jnp.float32(-1e30))
        maxima = jnp.max(scores, axis=1, keepdims=True)
        exponent = jnp.exp(scores - maxima)
        denominator = jnp.sum(exponent, axis=1, keepdims=True)
        weights = (exponent / denominator).astype(jnp.bfloat16)
        results.append(jnp.dot(weights, all_values, preferred_element_type=jnp.float32).astype(jnp.bfloat16))
    return jnp.concatenate(results, axis=1)


def reference(query, span_keys, span_values, cache_keys, stored_values, selected):
    query_group_count = QUERY_HEADS // KEY_VALUE_HEADS

    def one_block(block_index):
        begin_row = (block_index * BLOCK).astype(jnp.int32)
        results = []
        for key_value_head in range(KEY_VALUE_HEADS):
            query_group = lax.dynamic_slice(query, (begin_row, jnp.int32(key_value_head * query_group_count * HEAD_DIMENSION)), (BLOCK, query_group_count * HEAD_DIMENSION))
            key_list = [lax.dynamic_slice(span_keys, (begin_row, jnp.int32(key_value_head * HEAD_DIMENSION)), (BLOCK, HEAD_DIMENSION))]
            value_list = [lax.dynamic_slice(span_values, (begin_row, jnp.int32(key_value_head * HEAD_DIMENSION)), (BLOCK, HEAD_DIMENSION))]
            for slot_index in range(2):
                first_row = (selected[block_index, key_value_head, slot_index] * BLOCK).astype(jnp.int32)
                key_list.append(lax.dynamic_slice(cache_keys, (first_row, jnp.int32(key_value_head * HEAD_DIMENSION)), (BLOCK, HEAD_DIMENSION)))
                value_list.append(lax.dynamic_slice(stored_values, (first_row, jnp.int32(key_value_head * HEAD_DIMENSION)), (BLOCK, HEAD_DIMENSION)))
            results.append(attend(query_group, jnp.concatenate(key_list, axis=0), jnp.concatenate(value_list, axis=0), query_group_count))
        return jnp.concatenate(results, axis=1)

    blocks_out = lax.map(one_block, jnp.arange(QUERY_BLOCKS, dtype=jnp.int32))
    return blocks_out.reshape(SPAN_POSITIONS, QUERY_HEADS * HEAD_DIMENSION)
```

```python
import functools
import math

import jax
import jax.numpy as jnp
from jax import lax
from jax.experimental import pallas as pl
from jax.experimental.pallas import tpu as pltpu
from jax.sharding import PartitionSpec as P

QUERY_HEADS = 64
KEY_VALUE_HEADS = 8
HEAD = 128
GROUP = QUERY_HEADS // KEY_VALUE_HEADS
MESH = pl.DeviceIdType.MESH
CHUNK = 256


def partners(me, n):
    found = []
    if n & (n - 1) == 0:
        for t in range(n - 1, 0, -1):
            other = me
            for bit in range(n.bit_length()):
                if t >> bit & 1:
                    other = other + (1 << bit) * (1 - 2 * ((me // (1 << bit)) % 2))
            found.append((other, other))
    else:
        for t in range(1, n):
            found.append(((me + t) % n, (me + n - t) % n))
    return found


def kernel(n, kv, sel, query, span_keys, span_values, cache_keys, stored_values, out,
           qv, skv, svv, ckv, cvv, ov, all_sel, send, early, last, wide, acc, top,
           in_sem, out_sem, sel_send, sel_recv, send_sem, recv_sem):
    block = skv.shape[0]
    per_owner = ckv.shape[0] // block
    scale = HEAD ** (-0.5) * math.log2(math.e)
    me = lax.axis_index("ctx")
    others = partners(me, n)

    loads = [
        pltpu.make_async_copy(a, b, in_sem.at[i])
        for i, (a, b) in enumerate([
            (cache_keys, ckv), (stored_values, cvv), (query, qv),
            (span_keys, skv), (span_values, svv),
        ])
    ]
    for copy in loads:
        copy.start()

    barrier = pltpu.get_barrier_semaphore()
    for target, _ in others:
        pl.semaphore_signal(barrier, inc=1, device_id={"ctx": target}, device_id_type=MESH)
    pl.semaphore_wait(barrier, n - 1)

    sel_copies = []
    for j, (target, _) in enumerate(others):
        copy = pltpu.make_async_remote_copy(
            src_ref=sel, dst_ref=all_sel.at[j], send_sem=sel_send.at[j],
            recv_sem=sel_recv.at[j], device_id={"ctx": target}, device_id_type=MESH)
        copy.start()
        sel_copies.append(copy)

    def cols(h):
        return slice(h * HEAD, (h + 1) * HEAD)

    loads[0].wait()
    loads[1].wait()
    for copy in sel_copies:
        copy.wait()

    def held(first, second, cache, h):
        begin = me * per_owner
        found = cache[:block, cols(h)]
        for i in range(1, per_owner):
            wanted = (first == begin + i) | (second == begin + i)
            piece = cache[i * block:(i + 1) * block, cols(h)]
            found = jnp.where(jnp.full(found.shape, wanted), piece, found)
        return found

    remote = {}
    for h in range(kv):
        for j, (target, _) in enumerate(others):
            first, second = all_sel[j, 0, h, 0], all_sel[j, 0, h, 1]
            for kind, cache in enumerate((ckv, cvv)):
                send[h, j, kind] = held(first, second, cache, h)
                place = early[2 * h + kind].at[j + 1] if j < n - 2 else last[2 * h + kind]
                copy = pltpu.make_async_remote_copy(
                    src_ref=send.at[h, j, kind], dst_ref=place,
                    send_sem=send_sem.at[h, j, kind], recv_sem=recv_sem.at[h, j, kind],
                    device_id={"ctx": target}, device_id_type=MESH)
                copy.start()
                remote[h, j, kind] = copy
    for h in range(kv):
        for kind, cache in enumerate((ckv, cvv)):
            early[2 * h + kind][0] = held(sel[0, h, 0], sel[0, h, 1], cache, h)

    for copy in loads[2:]:
        copy.wait()
    wide[:, HEAD:] = jnp.ones((block, HEAD), jnp.bfloat16)

    def scores(rows, head, keys):
        return lax.dot_general(
            qv[rows, pl.ds(pl.multiple_of(head * HEAD, HEAD), HEAD)], keys,
            (((1,), (1,)), ((), ())), preferred_element_type=jnp.float32)

    def own(h):
        wide[:, :HEAD] = svv[:, cols(h)]

        @pl.loop(0, GROUP)
        def _(member):
            head = h * GROUP + member
            for start in range(0, block, CHUNK):
                rows, seen = slice(start, start + CHUNK), start + CHUNK
                s = scores(rows, head, skv[:seen, cols(h)])
                at = lax.broadcasted_iota(jnp.int32, (CHUNK, seen), 0) + start
                key = lax.broadcasted_iota(jnp.int32, (CHUNK, seen), 1)
                s = jnp.where(key <= at, s, -jnp.inf)
                m = jnp.max(s, axis=1, keepdims=True)
                p = jnp.exp2((s - m) * scale).astype(jnp.bfloat16)
                acc[head, rows] = jnp.dot(p, wide[:seen], preferred_element_type=jnp.float32)
                top[head, rows] = jnp.broadcast_to(m, (CHUNK, HEAD))

    def more(h, keys_ref, final):
        @pl.loop(0, GROUP)
        def _(member):
            head = h * GROUP + member
            for start in range(0, block, CHUNK):
                rows = slice(start, start + CHUNK)
                s = scores(rows, head, keys_ref[...])
                old = top[head, rows]
                m = jnp.maximum(old[:, :1], jnp.max(s, axis=1, keepdims=True))
                p = jnp.exp2((s - m) * scale).astype(jnp.bfloat16)
                shrink = jnp.exp2((old[:, :1] - m) * scale)
                total = acc[head, rows] * shrink + jnp.dot(
                    p, wide[...], preferred_element_type=jnp.float32)
                if final:
                    ov[rows, pl.ds(pl.multiple_of(head * HEAD, HEAD), HEAD)] = (
                        total[:, :HEAD] / total[:, HEAD:]).astype(jnp.bfloat16)
                else:
                    acc[head, rows] = total
                    top[head, rows] = jnp.broadcast_to(m, (CHUNK, HEAD))

    def owned(value, owner):
        begin = owner * per_owner
        return (value >= begin) & (value < begin + per_owner)

    def pick(tests, blocks):
        found = blocks[0][...]
        for test, other in zip(tests[1:], blocks[1:]):
            found = jnp.where(jnp.full(found.shape, test), other[...], found)
        return found

    owners = [me] + [source for _, source in others]
    for h in range(kv):
        own(h)
    stores = []
    for h in range(kv):
        first, second = sel[0, h, 0], sel[0, h, 1]
        swap = owned(first, owners[-1])
        one, two = jnp.where(swap, second, first), jnp.where(swap, first, second)
        for j in range(n - 2):
            for kind in range(2):
                remote[h, j, kind].wait_recv()
        picked_keys = skv.at[:, cols(h)]
        tests = [owned(one, owner) for owner in owners[:-1]]
        picked_keys[...] = pick(tests, [early[2 * h].at[i] for i in range(n - 1)])
        wide[:, :HEAD] = pick(tests, [early[2 * h + 1].at[i] for i in range(n - 1)])
        more(h, picked_keys, False)
        for kind in range(2):
            remote[h, n - 2, kind].wait_recv()
        tests = [owned(two, owner) for owner in owners]
        picked_keys[...] = pick(tests, [early[2 * h].at[i] for i in range(n - 1)] + [last[2 * h]])
        wide[:, :HEAD] = pick(
            tests, [early[2 * h + 1].at[i] for i in range(n - 1)] + [last[2 * h + 1]])
        more(h, picked_keys, True)
        columns = slice(h * GROUP * HEAD, (h + 1) * GROUP * HEAD)
        copy = pltpu.make_async_copy(ov.at[:, columns], out.at[:, columns], out_sem.at[h])
        copy.start()
        stores.append(copy)
    for copy in remote.values():
        copy.wait_send()
    for copy in stores:
        copy.wait()


def entry(n, kv, *refs):
    inputs, rest = refs[:7], list(refs[7:])
    head = rest[:8]
    rest = rest[8:]
    early, last, rest = rest[:2 * kv], rest[2 * kv:4 * kv], rest[4 * kv:]
    kernel(n, kv, *inputs, *head, early, last, *rest)


def per_device(n, query, span_keys, span_values, cache_keys, stored_values, selected):
    block, width = query.shape
    kv = span_keys.shape[1] // HEAD
    heads = width // HEAD
    bf, f32 = jnp.bfloat16, jnp.float32
    anywhere = pl.BlockSpec(memory_space=pl.ANY)
    dma = pltpu.SemaphoreType.DMA
    return pl.pallas_call(
        functools.partial(entry, n, kv),
        out_shape=jax.ShapeDtypeStruct(query.shape, bf),
        in_specs=[pl.BlockSpec(memory_space=pltpu.SMEM)] + [anywhere] * 5,
        out_specs=anywhere,
        scratch_shapes=[
            pltpu.VMEM(query.shape, bf),
            pltpu.VMEM(span_keys.shape, bf),
            pltpu.VMEM(span_values.shape, bf),
            pltpu.VMEM(cache_keys.shape, bf),
            pltpu.VMEM(stored_values.shape, bf),
            pltpu.VMEM(query.shape, bf),
            pltpu.SMEM((n - 1,) + selected.shape, jnp.int32),
            pltpu.VMEM((kv, n - 1, 2, block, HEAD), bf),
        ]
        + [pltpu.VMEM((n - 1, block, HEAD), bf)] * (2 * kv)
        + [pltpu.VMEM((block, HEAD), bf)] * (2 * kv)
        + [
            pltpu.VMEM((block, 2 * HEAD), bf),
            pltpu.VMEM((heads, block, 2 * HEAD), f32),
            pltpu.VMEM((heads, block, HEAD), f32),
            dma((5,)),
            dma((kv,)),
            dma((n - 1,)),
            dma((n - 1,)),
            dma((kv, n - 1, 2)),
            dma((kv, n - 1, 2)),
        ],
        compiler_params=pltpu.CompilerParams(
            collective_id=0, has_side_effects=True, vmem_limit_bytes=56 * 2**20),
        cost_estimate=pl.CostEstimate(
            flops=4 * block * 3 * block * width, bytes_accessed=6 * 2**20,
            transcendentals=heads * block * 3 * block),
    )(selected, query, span_keys, span_values, cache_keys, stored_values)


def solution(mesh):
    rows = P(("groups", "ctx"), "mp")
    return jax.shard_map(
        functools.partial(per_device, mesh.shape["ctx"]), mesh=mesh,
        in_specs=(rows,) * 5 + (P(("groups", "ctx"), "mp", None),),
        out_specs=rows, check_vma=False)
```

```python
import functools
import math

import jax
import jax.numpy as jnp
from jax import lax
from jax.experimental import pallas as pl
from jax.experimental.pallas import tpu as pltpu
from jax.sharding import PartitionSpec as P

QUERY_HEADS = 64
KEY_VALUE_HEADS = 8
HEAD = 128
GROUP = QUERY_HEADS // KEY_VALUE_HEADS
MESH = pl.DeviceIdType.MESH
CHUNK = 256


def partners(me, n):
    found = []
    if n & (n - 1) == 0:
        order = [1, 3, 2] if n == 4 else range(n - 1, 0, -1)
        for t in order:
            other = me
            for bit in range(n.bit_length()):
                if t >> bit & 1:
                    other = other + (1 << bit) * (1 - 2 * ((me // (1 << bit)) % 2))
            found.append((other, other))
    else:
        for t in range(1, n):
            found.append(((me + t) % n, (me + n - t) % n))
    return found


def sending(me, n, others):
    steps = [(j, target) for j, (target, _) in enumerate(others)]
    if n != 4:
        return steps
    inner = ((me + 1) % n) // 2
    near, far = others[0][0], others[2][0]
    return [
        (2 - 2 * inner, inner * near + (1 - inner) * far),
        steps[1],
        (2 * inner, (1 - inner) * near + inner * far),
    ]


def kernel(n, kv, sel, query, span_keys, span_values, cache_keys, stored_values, out,
           qv, skv, svv, ckv, cvv, ov, all_sel, send, got, wide, acc, top, probs,
           in_sem, out_sem, sel_send, sel_recv, send_sem, recv_sem):
    block = skv.shape[0]
    per_owner = ckv.shape[0] // block
    scale = HEAD ** (-0.5) * math.log2(math.e)
    me = lax.axis_index("ctx")
    others = partners(me, n)

    loads = [
        pltpu.make_async_copy(a, b, in_sem.at[i])
        for i, (a, b) in enumerate([
            (cache_keys, ckv), (stored_values, cvv), (query, qv),
            (span_keys, skv), (span_values, svv),
        ])
    ]
    for copy in loads:
        copy.start()

    barrier = pltpu.get_barrier_semaphore()
    for target, _ in others:
        pl.semaphore_signal(barrier, inc=1, device_id={"ctx": target}, device_id_type=MESH)
    pl.semaphore_wait(barrier, n - 1)

    sel_copies = []
    for j, (target, _) in enumerate(others):
        copy = pltpu.make_async_remote_copy(
            src_ref=sel, dst_ref=all_sel.at[j], send_sem=sel_send.at[j],
            recv_sem=sel_recv.at[j], device_id={"ctx": target}, device_id_type=MESH)
        copy.start()
        sel_copies.append(copy)

    def cols(h):
        return slice(h * HEAD, (h + 1) * HEAD)

    loads[0].wait()
    loads[1].wait()
    for copy in sel_copies:
        copy.wait()

    def held(first, second, cache, h):
        begin = me * per_owner
        found = cache[:block, cols(h)]
        for i in range(1, per_owner):
            wanted = (first == begin + i) | (second == begin + i)
            piece = cache[i * block:(i + 1) * block, cols(h)]
            found = jnp.where(jnp.full(found.shape, wanted), piece, found)
        return found

    def remote(h, j, kind, target):
        return pltpu.make_async_remote_copy(
            src_ref=send.at[h, j, kind], dst_ref=got.at[h, j, kind],
            send_sem=send_sem.at[h, j, kind], recv_sem=recv_sem.at[h, j, kind],
            device_id={"ctx": target}, device_id_type=MESH)

    for h in range(kv):
        for j, target in sending(me, n, others):
            first, second = all_sel[j, 0, h, 0], all_sel[j, 0, h, 1]
            for kind, cache in enumerate((ckv, cvv)):
                send[h, j, kind] = held(first, second, cache, h)
                remote(h, j, kind, target).start()
    for h in range(kv):
        for kind, cache in enumerate((ckv, cvv)):
            got[h, n - 1, kind] = held(sel[0, h, 0], sel[0, h, 1], cache, h)

    for copy in loads[2:]:
        copy.wait()
    wide[:, HEAD:] = jnp.ones((block, HEAD), jnp.bfloat16)

    def scores(rows, head, keys):
        return lax.dot_general(
            qv[rows, pl.ds(pl.multiple_of(head * HEAD, HEAD), HEAD)], keys,
            (((1,), (1,)), ((), ())), preferred_element_type=jnp.float32)

    def own(h):
        wide[:, :HEAD] = svv[:, cols(h)]

        @pl.loop(0, GROUP)
        def _(member):
            head = h * GROUP + member
            for start in range(0, block, CHUNK):
                rows, seen = slice(start, start + CHUNK), start + CHUNK
                s = scores(rows, head, skv[:seen, cols(h)])
                at = lax.broadcasted_iota(jnp.int32, (CHUNK, seen), 0) + start
                key = lax.broadcasted_iota(jnp.int32, (CHUNK, seen), 1)
                s = jnp.where(key <= at, s, -jnp.inf)
                m = jnp.max(s, axis=1, keepdims=True)
                p = jnp.exp2((s - m) * scale).astype(jnp.bfloat16)
                acc[head, rows] = jnp.dot(p, wide[:seen], preferred_element_type=jnp.float32)
                top[head, rows] = jnp.broadcast_to(m, (CHUNK, HEAD))

    def more(h, keys_ref, final):
        @pl.loop(0, GROUP)
        def _(member):
            head = h * GROUP + member
            for start in range(0, block, CHUNK):
                rows = slice(start, start + CHUNK)
                s = scores(rows, head, keys_ref[...])
                old = top[head, rows]
                m = jnp.maximum(old[:, :1], jnp.max(s, axis=1, keepdims=True))
                p = jnp.exp2((s - m) * scale).astype(jnp.bfloat16)
                shrink = jnp.exp2((old[:, :1] - m) * scale)
                total = acc[head, rows] * shrink + jnp.dot(
                    p, wide[...], preferred_element_type=jnp.float32)
                if final:
                    ov[rows, pl.ds(pl.multiple_of(head * HEAD, HEAD), HEAD)] = (
                        total[:, :HEAD] / total[:, HEAD:]).astype(jnp.bfloat16)
                else:
                    acc[head, rows] = total
                    top[head, rows] = jnp.broadcast_to(m, (CHUNK, HEAD))

    def weigh(h, keys_ref):
        @pl.loop(0, GROUP)
        def _(member):
            head = h * GROUP + member
            for start in range(0, block, CHUNK):
                rows = slice(start, start + CHUNK)
                s = scores(rows, head, keys_ref[...])
                old = top[head, rows]
                m = jnp.maximum(old[:, :1], jnp.max(s, axis=1, keepdims=True))
                probs[member, rows] = jnp.exp2((s - m) * scale).astype(jnp.bfloat16)
                acc[head, rows] = acc[head, rows] * jnp.exp2((old[:, :1] - m) * scale)

    def finish(h):
        @pl.loop(0, GROUP)
        def _(member):
            head = h * GROUP + member
            for start in range(0, block, CHUNK):
                rows = slice(start, start + CHUNK)
                total = acc[head, rows] + jnp.dot(
                    probs[member, rows], wide[...], preferred_element_type=jnp.float32)
                ov[rows, pl.ds(pl.multiple_of(head * HEAD, HEAD), HEAD)] = (
                    total[:, :HEAD] / total[:, HEAD:]).astype(jnp.bfloat16)

    def owned(value, owner):
        begin = owner * per_owner
        return (value >= begin) & (value < begin + per_owner)

    sources = [source for _, source in others]

    def pick(value, h, kind, slots):
        found = got[h, n - 1, kind]
        for j in slots:
            test = jnp.full(found.shape, owned(value, sources[j]))
            found = jnp.where(test, got[h, j, kind], found)
        return found

    def arrived(h, j, kind):
        remote(h, j, kind, others[j][0]).wait_recv()

    for h in range(kv):
        own(h)
    stores = []
    for h in range(kv):
        first, second = sel[0, h, 0], sel[0, h, 1]
        swap = owned(first, sources[-1])
        one, two = jnp.where(swap, second, first), jnp.where(swap, first, second)
        picked = skv.at[:, cols(h)]
        for kind in range(2):
            for j in range(n - 2):
                arrived(h, j, kind)
        picked[...] = pick(one, h, 0, range(n - 2))
        wide[:, :HEAD] = pick(one, h, 1, range(n - 2))
        more(h, picked, False)
        arrived(h, n - 2, 0)
        picked[...] = pick(two, h, 0, range(n - 1))
        if h == kv - 1:
            weigh(h, picked)
        arrived(h, n - 2, 1)
        wide[:, :HEAD] = pick(two, h, 1, range(n - 1))
        if h == kv - 1:
            finish(h)
        else:
            more(h, picked, True)
        columns = slice(h * GROUP * HEAD, (h + 1) * GROUP * HEAD)
        copy = pltpu.make_async_copy(ov.at[:, columns], out.at[:, columns], out_sem.at[h])
        copy.start()
        stores.append(copy)
    for h in range(kv):
        for j in range(n - 1):
            for kind in range(2):
                remote(h, j, kind, others[j][0]).wait_send()
    for copy in stores:
        copy.wait()


def per_device(n, query, span_keys, span_values, cache_keys, stored_values, selected):
    block, width = query.shape
    kv = span_keys.shape[1] // HEAD
    heads = width // HEAD
    bf, f32 = jnp.bfloat16, jnp.float32
    anywhere = pl.BlockSpec(memory_space=pl.ANY)
    dma = pltpu.SemaphoreType.DMA
    return pl.pallas_call(
        functools.partial(kernel, n, kv),
        out_shape=jax.ShapeDtypeStruct(query.shape, bf),
        in_specs=[pl.BlockSpec(memory_space=pltpu.SMEM)] + [anywhere] * 5,
        out_specs=anywhere,
        scratch_shapes=[
            pltpu.VMEM(query.shape, bf),
            pltpu.VMEM(span_keys.shape, bf),
            pltpu.VMEM(span_values.shape, bf),
            pltpu.VMEM(cache_keys.shape, bf),
            pltpu.VMEM(stored_values.shape, bf),
            pltpu.VMEM(query.shape, bf),
            pltpu.SMEM((n - 1,) + selected.shape, jnp.int32),
            pltpu.VMEM((kv, n - 1, 2, block, HEAD), bf),
            pltpu.VMEM((kv, n, 2, block, HEAD), bf),
            pltpu.VMEM((block, 2 * HEAD), bf),
            pltpu.VMEM((heads, block, 2 * HEAD), f32),
            pltpu.VMEM((heads, block, HEAD), f32),
            pltpu.VMEM((GROUP, block, block), bf),
            dma((5,)),
            dma((kv,)),
            dma((n - 1,)),
            dma((n - 1,)),
            dma((kv, n - 1, 2)),
            dma((kv, n - 1, 2)),
        ],
        compiler_params=pltpu.CompilerParams(
            collective_id=0, has_side_effects=True, vmem_limit_bytes=(28 + 8 * kv * n * block * HEAD // 2**20) * 2**20),
        cost_estimate=pl.CostEstimate(
            flops=4 * block * 3 * block * width, bytes_accessed=6 * 2**20,
            transcendentals=heads * block * 3 * block),
    )(selected, query, span_keys, span_values, cache_keys, stored_values)


def solution(mesh):
    rows = P(("groups", "ctx"), "mp")
    return jax.shard_map(
        functools.partial(per_device, mesh.shape["ctx"]), mesh=mesh,
        in_specs=(rows,) * 5 + (P(("groups", "ctx"), "mp", None),),
        out_specs=rows, check_vma=False)
```
